256 devices in a mesh: depth: 4 (over x), row: 8 (over z_hi, core), col: 8 (over z_lo, y).
Axes of the slice: x: 4, y: 4, z: 8 (z_hi: 4, z_lo: 2; z = z_hi * 2 + z_lo), core: 2. Of those that a mesh axis runs over, the one named last changes fastest.
Arguments:
- queries: bfloat16 [4096, 6144], P(('depth', 'col'), 'row'), may hold values from -7 to 7
- keys: bfloat16 [4096, 6144], P(('depth', 'col'), 'row'), may hold values from -7 to 7
- values: bfloat16 [4096, 6144], P(('depth', 'col'), 'row'), may hold values from -6 to 6
- out_weight: bfloat16 [6144, 12288], P('row', 'col'), may hold values from -0.078125 to 0.078125
- out_grad: bfloat16 [4096, 12288], P(('depth', 'row'), 'col'), may hold values from -3 to 3
Outputs:
- output: bfloat16 [4096, 12288], P(('depth', 'row'), 'col')
- query_grad: bfloat16 [4096, 6144], P(('depth', 'col'), 'row')
- key_grad: bfloat16 [4096, 6144], P(('depth', 'col'), 'row')
- value_grad: bfloat16 [4096, 6144], P(('depth', 'col'), 'row')
- weight_grad: bfloat16 [6144, 12288], P(('row', 'depth'), 'col')
The draws below stay inside these ranges and needn't reach their ends.
All inputs are finite; a program needn't handle non-finite values.
Results may differ from the reference program's by a relative error of at most 0.01.
Values may be sent and summed in bfloat16 or wider, within the bound.
No kernel may reach another device: no remote copies, remote signals or barrier semaphores. Data moves between devices by JAX's collectives and lax.ppermute only.
A program may use at most 128 MiB of HBM per device.

```python
import math
import jax
import jax.numpy as jnp
from jax import lax

D = 12288
DH = 128
HEADS = 48
HD = 6144
SEQ = 1024
TOKENS = 4096
N_DEPTH = 4


def draw_queries(key, part):
    key = jax.random.fold_in(key, 11)
    drawn = jnp.clip(jax.random.normal(key, (TOKENS, HD), jnp.float32), -6.0, 6.0)
    return drawn.astype(jnp.bfloat16)


def draw_keys(key, part):
    key = jax.random.fold_in(key, 12)
    drawn = jnp.clip(jax.random.normal(key, (TOKENS, HD), jnp.float32), -6.0, 6.0)
    return drawn.astype(jnp.bfloat16)


def steps_of(stream_key, extent, split, smallest, top_value):
    factor_of = 1.0
    for dim, shards_of in split:
        draws = jax.random.uniform(jax.random.fold_in(jax.random.fold_in(stream_key, 6), dim), (shards_of,), jnp.float32, smallest / len(split), top_value / len(split))
        factor_of = factor_of * jnp.repeat(jnp.exp(draws), extent[dim] // shards_of).reshape((-1,) + (1,) * (len(extent) - 1 - dim))
    return factor_of


def centred(own_key, shape, spread, most, pieces=(), kind=jnp.bfloat16):
    gain = steps_of(own_key, shape, pieces, -0.22, 0.18) if pieces else 1.0
    result = jax.random.normal(own_key, shape, jnp.float32) * spread * gain
    return jnp.minimum(jnp.maximum(result, -most), most).astype(kind)


def setup_inputs(seed: int = 0) -> dict:
    arg_keys = jax.random.split(jax.random.key(seed), 6)
    queries = draw_queries(jax.random.fold_in(arg_keys[5], 71), 0)
    keys = draw_keys(jax.random.fold_in(arg_keys[5], 71), 0)
    values = centred(arg_keys[2], (TOKENS, HD), 1.0, 6.0, ((0, 32), (1, 8)))
    out_weight = centred(arg_keys[3], (HD, D), HD ** -0.5, 0.078125, ((0, 8), (1, 8)))
    out_grad = centred(arg_keys[4], (TOKENS, D), 0.5, 3.0, ((0, 32), (1, 8)))
    return dict(queries=queries, keys=keys, values=values, out_weight=out_weight, out_grad=out_grad)


def heads_first(array):
    return array.reshape(N_DEPTH, SEQ, HEADS, DH).transpose(0, 2, 1, 3).reshape(N_DEPTH * HEADS, SEQ, DH)

def heads_back(array):
    return array.reshape(N_DEPTH, HEADS, SEQ, DH).transpose(0, 2, 1, 3).reshape(N_DEPTH * SEQ, HEADS * DH)

def attend_rows(query_block, key_block):
    scores = jnp.dot(query_block, key_block.T, preferred_element_type=jnp.float32) * (1.0 / math.sqrt(DH))
    places = jnp.arange(SEQ, dtype=jnp.int32)
    scores = jnp.where(places[:, None] >= places[None, :], scores, -jnp.inf)
    row_top = lax.optimization_barrier(jnp.max(scores, axis=-1, keepdims=True))
    shifted = jnp.exp(scores - row_top)
    return shifted / lax.optimization_barrier(jnp.sum(shifted, axis=-1, keepdims=True))

def forward_head(items):
    query_block, key_block, value_block = items
    attend = attend_rows(query_block, key_block)
    attend_low = attend.astype(jnp.bfloat16)
    return jnp.dot(attend_low, value_block, preferred_element_type=jnp.float32).astype(jnp.bfloat16)

def backward_head(items):
    query_block, key_block, value_block, grad_block = items
    score_scale = 1.0 / math.sqrt(DH)
    attend = attend_rows(query_block, key_block)
    attend_low = attend.astype(jnp.bfloat16)
    value_part = jnp.dot(attend_low.T, grad_block, preferred_element_type=jnp.float32).astype(jnp.bfloat16)
    prob_grad = jnp.dot(grad_block, value_block.T, preferred_element_type=jnp.float32)
    row_dot = lax.optimization_barrier(jnp.sum(attend * prob_grad, axis=-1, keepdims=True))
    score_grad = (attend * (prob_grad - row_dot) * score_scale).astype(jnp.bfloat16)
    query_part = jnp.dot(score_grad, key_block, preferred_element_type=jnp.float32).astype(jnp.bfloat16)
    key_part = jnp.dot(score_grad.T, query_block, preferred_element_type=jnp.float32).astype(jnp.bfloat16)
    return (query_part, key_part, value_part)

def reference(queries, keys, values, out_weight, out_grad):
    query_heads = heads_first(queries)
    key_heads = heads_first(keys)
    value_heads = heads_first(values)
    context = heads_back(lax.map(forward_head, (query_heads, key_heads, value_heads)))
    output = jnp.dot(context, out_weight, preferred_element_type=jnp.float32).astype(jnp.bfloat16)
    context_grad = jnp.dot(out_grad, out_weight.T, preferred_element_type=jnp.float32).astype(jnp.bfloat16)
    weight_grad = jnp.dot(context.T, out_grad, preferred_element_type=jnp.float32).astype(jnp.bfloat16)
    query_part, key_part, value_part = lax.map(backward_head, (query_heads, key_heads, value_heads, heads_first(context_grad)))
    return (output, heads_back(query_part), heads_back(key_part), heads_back(value_part), weight_grad)
```

```python
import functools
import math

import jax
import jax.numpy as jnp
from jax import lax
from jax.experimental import pallas as pl
from jax.experimental.pallas import tpu as pltpu
from jax.sharding import PartitionSpec as P

DH = 128
POS = 128
QB = 256
SCALE = 1.0 / math.sqrt(DH)
F32 = jnp.float32
BF16 = jnp.bfloat16
VMEM = pl.BlockSpec(memory_space=pltpu.VMEM)
PARAMS = pltpu.CompilerParams(vmem_limit_bytes=40 * 1024 * 1024)

NT = (((1,), (1,)), ((), ()))
TN = (((0,), (0,)), ((), ()))


def along_h(step):
    return [(2 * h + k, 2 * ((h + step) % 4) + k) for h in range(4) for k in range(2)]


ACROSS_CORE = [(r, r ^ 1) for r in range(8)]
ACROSS_Z = [(4 * z + y, 4 * (1 - z) + y) for z in range(2) for y in range(3)]


def from_owner(step):
    return [(4 * z + y, 4 * z + (y + step) % 4) for z in range(2) for y in range(3)]


def to_owner(step):
    return [
        (4 * z + y, 4 * z + (y + step) % 4)
        for z in range(2)
        for y in range(4)
        if (y + step) % 4 < 3
    ]


def attend_block(q, k, first):
    keys = k.shape[0]
    s = lax.dot_general(q, k, NT, preferred_element_type=F32) * SCALE
    rows = first + lax.broadcasted_iota(jnp.int32, (QB, keys), 0)
    cols = lax.broadcasted_iota(jnp.int32, (QB, keys), 1)
    s = jnp.where(rows >= cols, s, -jnp.inf)
    p = jnp.exp(s - jnp.max(s, axis=-1, keepdims=True))
    return p / jnp.sum(p, axis=-1, keepdims=True)


def forward_kernel(qkv, ctx):
    for i in range(qkv.shape[0] // QB):
        rows, seen = pl.ds(i * QB, QB), pl.ds(0, (i + 1) * QB)
        low = attend_block(qkv[rows, :DH], qkv[seen, DH : 2 * DH], i * QB).astype(BF16)
        ctx[rows, :] = jnp.dot(low, qkv[seen, 2 * DH :], preferred_element_type=F32).astype(BF16)


def backward_kernel(qkv, grad, out, dk, dv):
    blocks = qkv.shape[0] // QB
    for i in reversed(range(blocks)):
        rows, seen = pl.ds(i * QB, QB), pl.ds(0, (i + 1) * QB)
        q, k, v, g = qkv[rows, :DH], qkv[seen, DH : 2 * DH], qkv[seen, 2 * DH :], grad[rows, :]
        attend = attend_block(q, k, i * QB)
        dp = lax.dot_general(g, v, NT, preferred_element_type=F32)
        dot = jnp.sum(attend * dp, axis=-1, keepdims=True)
        ds = (attend * (dp - dot) * SCALE).astype(BF16)
        out[rows, :DH] = jnp.dot(ds, k, preferred_element_type=F32).astype(BF16)
        dk_part = lax.dot_general(ds, q, TN, preferred_element_type=F32)
        dv_part = lax.dot_general(attend.astype(BF16), g, TN, preferred_element_type=F32)
        if i == blocks - 1:
            dk[...] = dk_part
            dv[...] = dv_part
        else:
            dk[seen, :] += dk_part
            dv[seen, :] += dv_part
    out[:, DH : 2 * DH] = dk[...].astype(BF16)
    out[:, 2 * DH :] = dv[...].astype(BF16)


def forward(qkv):
    seq = qkv.shape[0]
    return pl.pallas_call(
        forward_kernel,
        out_shape=jax.ShapeDtypeStruct((seq, DH), BF16),
        in_specs=[VMEM],
        out_specs=VMEM,
        compiler_params=PARAMS,
        cost_estimate=pl.CostEstimate(
            flops=3 * seq * seq * DH, bytes_accessed=seq * DH * 8, transcendentals=seq * seq
        ),
        name="attend_forward",
    )(qkv)


def backward(qkv, grad):
    seq = qkv.shape[0]
    return pl.pallas_call(
        backward_kernel,
        out_shape=jax.ShapeDtypeStruct((seq, 3 * DH), BF16),
        in_specs=[VMEM, VMEM],
        out_specs=VMEM,
        scratch_shapes=[pltpu.VMEM((seq, DH), F32), pltpu.VMEM((seq, DH), F32)],
        compiler_params=PARAMS,
        cost_estimate=pl.CostEstimate(
            flops=7 * seq * seq * DH, bytes_accessed=seq * DH * 14, transcendentals=seq * seq
        ),
        name="attend_backward",
    )(qkv, grad)


def shards(queries, keys, values, weight, out_grad):
    row, col, d = lax.axis_index("row"), lax.axis_index("col"), lax.axis_index("depth")
    h, core = row // 2, row % 2
    z, y = col // 4, col % 4
    feats = weight.shape[1]
    half = feats // 2
    on_row = lambda a, perm: lax.ppermute(a, "row", perm)
    on_col = lambda a, perm: lax.ppermute(a, "col", perm)

    stacked = jnp.stack([a.reshape(POS, 6, DH) for a in (queries, keys, values)], axis=2)
    by_head = stacked.transpose(1, 0, 2, 3).reshape(6, POS, 3 * DH)
    none = jnp.zeros((1, POS, 3 * DH), BF16)
    slots = jnp.concatenate([by_head[:3], none, by_head[3:], none], axis=0)

    g_before = on_row(out_grad, along_h(1))
    g_after = on_row(out_grad, along_h(-1))
    qkv = lax.all_to_all(slots, "col", 0, 0, tiled=True).reshape(8 * POS, 3 * DH)
    far_a = on_row(g_before[:, :half], along_h(1))
    far_b = on_row(g_after[:, half:], along_h(-1))
    g_far = jnp.concatenate([far_a, far_b], axis=1)
    grad_all = jnp.zeros((4, 2, POS, feats), BF16)
    for block, shift in ((out_grad, 0), (g_before, 3), (g_after, 1), (g_far, 2)):
        other = on_row(block, ACROSS_CORE)
        place = (h + shift) % 4
        grad_all = lax.dynamic_update_slice(grad_all, block[None, None], (place, core, 0, 0))
        grad_all = lax.dynamic_update_slice(grad_all, other[None, None], (place, 1 - core, 0, 0))
    grad_all = grad_all.reshape(8 * POS, feats)

    w_heads = weight.reshape(6, DH, feats)
    w_rel = []
    for t in range(4):
        for b in range(2):
            head = 3 * (z ^ b) + jnp.minimum((y + t) % 4, 2)
            w_rel.append(lax.dynamic_slice_in_dim(w_heads, head, 1, 0))
    w_rel = jnp.concatenate(w_rel, axis=0).reshape(8 * DH, feats)

    ctx = forward(qkv)
    ctx_z = on_col(ctx, ACROSS_Z)
    pairs = [None] * 4
    pairs[0] = (ctx, ctx_z)
    near = [on_col(ctx, from_owner(s)) for s in (1, 2, 3)]
    across = [on_col(ctx_z, from_owner(s)) for s in (1, 2, 3)]
    for s in (1, 2, 3):
        pairs[4 - s] = (near[s - 1], across[s - 1])
    ctx_rel = jnp.concatenate([a for pair in pairs for a in pair], axis=1)

    sends = []
    for t in (1, 2, 3):
        part = lax.dot_general(
            grad_all, w_rel[2 * DH * t : 2 * DH * (t + 1)], NT, preferred_element_type=F32
        ).astype(BF16)
        sends.append(on_col(part, to_owner(t)))
    total = lax.dot_general(grad_all, w_rel[: 2 * DH], NT, preferred_element_type=F32)
    for part in sends:
        total = total + part.astype(F32)
    from_z = on_col(total[:, DH:].astype(BF16), ACROSS_Z)
    grad = (total[:, :DH] + from_z.astype(F32)).astype(BF16)

    blocks = ctx_rel.reshape(4, 2, POS, 8 * DH)

    def rows_of(k):
        picked = [
            lax.dynamic_slice(blocks, ((h + s) % 4, k, 0, 0), (1, 1, POS, 8 * DH)).reshape(
                POS, 8 * DH
            )
            for s in (2, 1, 3, 0)
        ]
        return jnp.concatenate(picked, axis=0)

    theirs = jnp.dot(rows_of(1 - core), w_rel, preferred_element_type=F32).astype(BF16)
    mine = jnp.dot(rows_of(core), w_rel, preferred_element_type=F32)
    mine = mine + on_row(theirs, ACROSS_CORE).astype(F32)
    far, up, down, own = [mine[POS * i : POS * (i + 1)] for i in range(4)]
    a = on_row(far[:, :half].astype(BF16), along_h(1))
    b = on_row(far[:, half:].astype(BF16), along_h(-1))
    up_b = on_row(up[:, half:].astype(BF16), along_h(1))
    down_a = on_row(down[:, :half].astype(BF16), along_h(-1))
    up_a = on_row((up[:, :half] + a.astype(F32)).astype(BF16), along_h(1))
    down_b = on_row((down[:, half:] + b.astype(F32)).astype(BF16), along_h(-1))
    output = jnp.concatenate(
        [
            own[:, :half] + up_a.astype(F32) + down_a.astype(F32),
            own[:, half:] + up_b.astype(F32) + down_b.astype(F32),
        ],
        axis=1,
    ).astype(BF16)

    w_part = lax.dot_general(ctx_rel, grad_all, TN, preferred_element_type=F32).astype(BF16)
    w_part = w_part.reshape(8, 2, DH // 2, feats)

    def share(target):
        picked = []
        for i in range(3):
            unit = target * 3 + i
            head = unit // 2
            hz, hy = head // 3, head % 3
            place = 2 * ((hy - y) % 4) + (hz ^ z)
            picked.append(
                lax.dynamic_slice(
                    w_part, (place, unit % 2, 0, 0), (1, 1, DH // 2, feats)
                ).reshape(DH // 2, feats)
            )
        return jnp.concatenate(picked, axis=0)

    weight_grad = share(d).astype(F32)
    for s in (1, 2, 3):
        moved = lax.ppermute(share((d + s) % 4), "depth", [(i, (i + s) % 4) for i in range(4)])
        weight_grad = weight_grad + moved.astype(F32)
    weight_grad = weight_grad.astype(BF16)

    back = backward(qkv, grad).reshape(8, POS, 3 * DH)
    back = lax.all_to_all(back, "col", 0, 0, tiled=True)
    back = jnp.concatenate([back[:3], back[4:7]], axis=0)
    grads = [
        back[:, :, DH * i : DH * (i + 1)].transpose(1, 0, 2).reshape(POS, 6 * DH) for i in range(3)
    ]
    return output, grads[0], grads[1], grads[2], weight_grad


def solution(mesh):
    in_specs = (
        P(("depth", "col"), "row"),
        P(("depth", "col"), "row"),
        P(("depth", "col"), "row"),
        P("row", "col"),
        P(("depth", "row"), "col"),
    )
    out_specs = (
        P(("depth", "row"), "col"),
        P(("depth", "col"), "row"),
        P(("depth", "col"), "row"),
        P(("depth", "col"), "row"),
        P(("row", "depth"), "col"),
    )
    return jax.shard_map(shards, mesh=mesh, in_specs=in_specs, out_specs=out_specs, check_vma=False)
```

```python
import math

import jax
import jax.numpy as jnp
from jax import lax
from jax.experimental import pallas as pl
from jax.experimental.pallas import tpu as pltpu
from jax.sharding import PartitionSpec as P

DH = 128
POS = 128
QB = 256
SCALE = 1.0 / math.sqrt(DH)
F32 = jnp.float32
BF16 = jnp.bfloat16
NT = (((1,), (1,)), ((), ()))
TN = (((0,), (0,)), ((), ()))

OWNERS = (0, 1, 2, 4, 5, 6)

SAME_Z = [[0, 1, 2, 3], [4, 5, 6, 7]]
ACROSS_Z = [(c, (c + 4) % 8) for c in range(8)]
ACROSS_CORE = [(r, r ^ 1) for r in range(8)]


def by_core(step):
    return [(2 * h + k, 2 * ((h + step * (1 - 2 * k)) % 4) + k) for h in range(4) for k in range(2)]


ARRAY = jax.ShapeDtypeStruct
IN_HBM = pltpu.HBM
HBM = pl.BlockSpec(memory_space=pltpu.HBM)
WHOLE = pl.BlockSpec(memory_space=pltpu.VMEM)


def local(kernel, name, outs, args, out_specs=None, in_specs=None, grid=(), scratch=(), after=(), flops=1024, vmem=56):
    count = len(args)

    def body(*refs):
        kernel(*refs[:count], *refs[count + len(after) :])

    return pl.pallas_call(
        body,
        out_shape=[kind(shape, dtype) for shape, dtype, kind in outs],
        grid=grid,
        in_specs=list(in_specs or [WHOLE] * count)
        + [pl.BlockSpec(memory_space=pl.ANY)] * len(after),
        out_specs=list(out_specs or [WHOLE] * len(outs)),
        scratch_shapes=list(scratch),
        compiler_params=pltpu.CompilerParams(vmem_limit_bytes=vmem * 1024 * 1024),
        cost_estimate=pl.CostEstimate(flops=flops, bytes_accessed=1024, transcendentals=0),
        name=name,
    )(*args, *after)


def pack_kernel(q, k, v, slots):
    for j, slot in enumerate(OWNERS):
        for i, a in enumerate((q, k, v)):
            slots[slot, :, i * DH : (i + 1) * DH] = a[:, j * DH : (j + 1) * DH]
    for slot in (3, 7):
        slots[slot] = jnp.zeros(slots.shape[1:], slots.dtype)


def unpack_kernel(slots, q, k, v):
    for j, slot in enumerate(OWNERS):
        for i, a in enumerate((q, k, v)):
            a[:, j * DH : (j + 1) * DH] = slots[slot, :, i * DH : (i + 1) * DH]


def attend_block(q, k, first):
    keys = k.shape[0]
    s = lax.dot_general(q, k, NT, preferred_element_type=F32) * SCALE
    rows = first + lax.broadcasted_iota(jnp.int32, (QB, keys), 0)
    cols = lax.broadcasted_iota(jnp.int32, (QB, keys), 1)
    s = jnp.where(rows >= cols, s, -jnp.inf)
    p = jnp.exp(s - jnp.max(s, axis=-1, keepdims=True))
    return p / jnp.sum(p, axis=-1, keepdims=True)


def forward_kernel(qkv, copies, ctx, sems):
    blocks = qkv.shape[0] // QB
    out = []
    for i in range(blocks):
        rows, seen = pl.ds(i * QB, QB), pl.ds(0, (i + 1) * QB)
        low = attend_block(qkv[rows, :DH], qkv[seen, DH : 2 * DH], i * QB).astype(BF16)
        ctx[rows, :] = jnp.dot(low, qkv[seen, 2 * DH :], preferred_element_type=F32).astype(BF16)
        for c in range(copies.shape[0]):
            out.append(
                pltpu.make_async_copy(ctx.at[rows, :], copies.at[c, rows, :], sems.at[i, c])
            )
            out[-1].start()
    for copy in out:
        copy.wait()


def backward_kernel(qkv, parts, out, dk, dv):
    blocks = qkv.shape[0] // QB
    step = pl.program_id(0)

    for i in reversed(range(blocks)):

        @pl.when(step == blocks - 1 - i)
        def _(i=i):
            rows, seen = pl.ds(i * QB, QB), pl.ds(0, (i + 1) * QB)
            q, k, v = qkv[rows, :DH], qkv[seen, DH : 2 * DH], qkv[seen, 2 * DH :]
            g = parts[0].astype(F32)
            for c in range(1, parts.shape[0]):
                g = g + parts[c].astype(F32)
            g = g.astype(BF16)
            attend = attend_block(q, k, i * QB)
            dp = lax.dot_general(g, v, NT, preferred_element_type=F32)
            dot = jnp.sum(attend * dp, axis=-1, keepdims=True)
            ds = (attend * (dp - dot) * SCALE).astype(BF16)
            out[rows, :DH] = jnp.dot(ds, k, preferred_element_type=F32).astype(BF16)
            dk_part = lax.dot_general(ds, q, TN, preferred_element_type=F32)
            dv_part = lax.dot_general(attend.astype(BF16), g, TN, preferred_element_type=F32)
            if i == blocks - 1:
                dk[...] = dk_part
                dv[...] = dv_part
            else:
                dk[seen, :] += dk_part
                dv[seen, :] += dv_part
            out[rows, DH : 2 * DH] = dk[rows, :].astype(BF16)
            out[rows, 2 * DH :] = dv[rows, :].astype(BF16)


def context_grad_kernel(grad_all, w, slots, token, part, sems):
    token[...] = jnp.zeros(token.shape, token.dtype)
    leave = []
    for j in range(0, 6, 2):
        both = lax.dot_general(
            grad_all[...], w[j * DH : (j + 2) * DH, :], NT, preferred_element_type=F32
        ).astype(BF16)
        for k in range(2):
            part[j + k] = both[:, k * DH : (k + 1) * DH]
            leave.append(
                pltpu.make_async_copy(part.at[j + k], slots.at[OWNERS[j + k]], sems.at[j + k])
            )
            leave[-1].start()
    for copy in leave:
        copy.wait()


def rows_for(ctx, h, core):
    first = [pl.multiple_of((2 * lax.rem(h + s, 4) + core) * POS, POS) for s in (2, 1, 3, 0)]
    return jnp.concatenate([ctx[pl.ds(f, POS), :] for f in first], axis=0)


def theirs_kernel(place, near, other, weight, ctx, left, right, w, sems_in, sems_w):
    h, core, z = place[0], place[1], place[2]
    wide = left.shape[1]
    lanes = [pl.ds(i * wide, wide) for i in range(2)]
    arrive = []
    for i, (blocks, zz) in enumerate(((near, z), (other, 1 - z))):
        for y in range(3):
            first = pl.multiple_of((3 * zz + y) * DH, DH)
            arrive.append(
                pltpu.make_async_copy(blocks.at[y], ctx.at[:, pl.ds(first, DH)], sems_in.at[i, y])
            )
    weights = [
        pltpu.make_async_copy(weight.at[:, lane], w.at[:, lane], sems_w.at[i])
        for i, lane in enumerate(lanes)
    ]
    for copy in arrive + weights:
        copy.start()
    for copy in arrive:
        copy.wait()
    rows = rows_for(ctx, h, 1 - core)
    for i, out in enumerate((left, right)):
        weights[i].wait()
        out[...] = jnp.dot(rows, w[:, lanes[i]], preferred_element_type=F32).astype(BF16)


def mine_kernel(place, ctx, w, left, right, far, now, later, own):
    h, core = place[0], place[1]
    rows = rows_for(ctx, h, core)
    wide = left.shape[1]
    for i, theirs in enumerate((left, right)):
        lane = pl.ds(i * wide, wide)
        part = jnp.dot(rows, w[:, lane], preferred_element_type=F32)
        part = part + theirs[...].astype(F32)
        far[:, lane] = part[:POS].astype(BF16)
        up, down = part[POS : 2 * POS], part[2 * POS : 3 * POS]
        now[:, lane] = jnp.where(core == 0, down, up).astype(BF16)
        later[:, lane] = jnp.where(core == 0, up, down)
        own[:, lane] = part[3 * POS :]


def add_kernel(a, *parts):
    total = a[...]
    for part in parts[:-1]:
        total = total + part[...].astype(F32)
    parts[-1][...] = total.astype(BF16)


def weight_kernel(ctx, grad_all, out, token):
    token[...] = jnp.zeros(token.shape, token.dtype)
    out[...] = lax.dot_general(
        ctx[...], grad_all[...], TN, preferred_element_type=F32
    ).astype(out.dtype)


def shards(queries, keys, values, weight, out_grad):
    feats = weight.shape[1]
    seq = 8 * POS
    width = 6 * DH
    steps = seq // QB
    row, col = lax.axis_index("row"), lax.axis_index("col")
    place = jnp.stack([row // 2, row % 2, col // 4]).astype(jnp.int32)
    on_row = lambda a, perm: lax.ppermute(a, "row", perm)
    scalars = pl.BlockSpec(memory_space=pltpu.SMEM)
    trade = lambda a: lax.all_to_all(a, "col", 0, 0, tiled=True)
    whole = lambda shape: pl.BlockSpec(shape, lambda i: (0,) * len(shape))
    lanes_of = lambda rows: pl.BlockSpec((rows, 512), lambda i: (0, i))

    grad_all = lax.all_gather(out_grad, "row", axis=0, tiled=True)

    (slots,) = local(
        pack_kernel, "pack_heads", [((8, POS, 3 * DH), BF16, IN_HBM)], (queries, keys, values)
    )
    qkv = trade(slots).reshape(seq, 3 * DH)

    (copies,) = local(
        forward_kernel,
        "attend_forward",
        [((4, seq, DH), BF16, IN_HBM)],
        (qkv,),
        out_specs=[HBM],
        scratch=[pltpu.VMEM((seq, DH), BF16), pltpu.SemaphoreType.DMA((steps, 4))],
    )
    near = lax.all_to_all(copies, "col", 0, 0, tiled=True, axis_index_groups=SAME_Z)
    other = lax.ppermute(near[:3], "col", ACROSS_Z)

    parts, token = local(
        context_grad_kernel,
        "context_grad",
        [((8, seq, DH), BF16, IN_HBM), ((8, DH), F32, ARRAY)],
        (grad_all, weight),
        out_specs=[HBM, WHOLE],
        scratch=[pltpu.VMEM((6, seq, DH), BF16), pltpu.SemaphoreType.DMA((6,))],
        vmem=24,
    )
    parts = trade(parts)

    ctx, *theirs = local(
        theirs_kernel,
        "project_theirs",
        [((seq, width), BF16, ARRAY)] + [((seq // 2, feats // 2), BF16, ARRAY)] * 2,
        (place, near, other, weight),
        in_specs=[scalars, HBM, HBM, HBM],
        scratch=[
            pltpu.VMEM((width, feats), BF16),
            pltpu.SemaphoreType.DMA((2, 3)),
            pltpu.SemaphoreType.DMA((2,)),
        ],
        after=[token],
        flops=60_000_000_000,
    )
    w_part, token = local(
        weight_kernel,
        "weight_grad",
        [((width, feats), BF16, ARRAY), ((8, DH), F32, ARRAY)],
        (ctx, grad_all),
        vmem=24,
        grid=(feats // 512,),
        in_specs=[whole((seq, width)), lanes_of(seq)],
        out_specs=[lanes_of(width), whole((8, DH))],
    )
    weight_grad = lax.psum_scatter(w_part, "depth", scatter_dimension=0, tiled=True)

    block = (POS, feats)
    far, now, later, own = local(
        mine_kernel,
        "project_mine",
        [(block, BF16, ARRAY), (block, BF16, ARRAY), (block, F32, ARRAY), (block, F32, ARRAY)],
        (place, ctx, weight, *[on_row(a, ACROSS_CORE) for a in theirs]),
        in_specs=[scalars] + [WHOLE] * 4,
        after=[token],
        vmem=24,
    )
    far = on_row(far, by_core(1))
    now = on_row(now, by_core(-1))
    (later,) = local(add_kernel, "add_output", [(block, BF16, ARRAY)], (later, far), flops=60_000_000_000, vmem=24)
    later = on_row(later, by_core(1))
    (output,) = local(
        add_kernel,
        "sum_output",
        [(block, BF16, ARRAY)],
        (own, now, later),
        vmem=24,
    )

    (back,) = local(
        backward_kernel,
        "attend_backward",
        [((seq, 3 * DH), BF16, IN_HBM)],
        (qkv, parts),
        after=[own],
        vmem=24,
        grid=(steps,),
        in_specs=[
            whole((seq, 3 * DH)),
            pl.BlockSpec((8, QB, DH), lambda i: (0, steps - 1 - i, 0)),
        ],
        out_specs=[whole((seq, 3 * DH))],
        scratch=[pltpu.VMEM((seq, DH), F32), pltpu.VMEM((seq, DH), F32)],
    )
    back = trade(back.reshape(8, POS, 3 * DH))
    grads = local(unpack_kernel, "unpack_heads", [((POS, width), BF16, ARRAY)] * 3, (back,), vmem=24)

    return output, grads[0], grads[1], grads[2], weight_grad


def solution(mesh):
    in_specs = (
        P(("depth", "col"), "row"),
        P(("depth", "col"), "row"),
        P(("depth", "col"), "row"),
        P("row", "col"),
        P(("depth", "row"), "col"),
    )
    out_specs = (
        P(("depth", "row"), "col"),
        P(("depth", "col"), "row"),
        P(("depth", "col"), "row"),
        P(("depth", "col"), "row"),
        P(("row", "depth"), "col"),
    )
    return jax.shard_map(shards, mesh=mesh, in_specs=in_specs, out_specs=out_specs, check_vma=False)
```

```python
import math

import jax
import jax.numpy as jnp
from jax import lax
from jax.experimental import pallas as pl
from jax.experimental.pallas import tpu as pltpu
from jax.sharding import PartitionSpec as P

DH = 128
POS = 128
QB = 256
SCALE = 1.0 / math.sqrt(DH)
F32 = jnp.float32
BF16 = jnp.bfloat16
NT = (((1,), (1,)), ((), ()))
TN = (((0,), (0,)), ((), ()))

OWNERS = (0, 1, 2, 4, 5, 6)

SAME_Z = [[0, 1, 2, 3], [4, 5, 6, 7]]
ACROSS_Z = [(c, (c + 4) % 8) for c in range(8)]
ACROSS_CORE = [(r, r ^ 1) for r in range(8)]


def by_core(step):
    return [(2 * h + k, 2 * ((h + step * (1 - 2 * k)) % 4) + k) for h in range(4) for k in range(2)]


ARRAY = jax.ShapeDtypeStruct
IN_HBM = pltpu.HBM
HBM = pl.BlockSpec(memory_space=pltpu.HBM)
WHOLE = pl.BlockSpec(memory_space=pltpu.VMEM)


def local(kernel, name, outs, args, out_specs=None, in_specs=None, grid=(), scratch=(), after=(), flops=1024, vmem=56):
    count = len(args)

    def body(*refs):
        kernel(*refs[:count], *refs[count + len(after) :])

    return pl.pallas_call(
        body,
        out_shape=[kind(shape, dtype) for shape, dtype, kind in outs],
        grid=grid,
        in_specs=list(in_specs or [WHOLE] * count)
        + [pl.BlockSpec(memory_space=pl.ANY)] * len(after),
        out_specs=list(out_specs or [WHOLE] * len(outs)),
        scratch_shapes=list(scratch),
        compiler_params=pltpu.CompilerParams(vmem_limit_bytes=vmem * 1024 * 1024),
        cost_estimate=pl.CostEstimate(flops=flops, bytes_accessed=1024, transcendentals=0),
        name=name,
    )(*args, *after)


def pack_kernel(q, k, v, slots):
    for j, slot in enumerate(OWNERS):
        for i, a in enumerate((q, k, v)):
            slots[slot, :, i * DH : (i + 1) * DH] = a[:, j * DH : (j + 1) * DH]
    for slot in (3, 7):
        slots[slot] = jnp.zeros(slots.shape[1:], slots.dtype)


def unpack_kernel(slots, q, k, v):
    for j, slot in enumerate(OWNERS):
        for i, a in enumerate((q, k, v)):
            a[:, j * DH : (j + 1) * DH] = slots[slot, :, i * DH : (i + 1) * DH]


def attend_block(q, k, first):
    keys = k.shape[0]
    s = lax.dot_general(q, k, NT, preferred_element_type=F32) * SCALE
    rows = first + lax.broadcasted_iota(jnp.int32, (QB, keys), 0)
    cols = lax.broadcasted_iota(jnp.int32, (QB, keys), 1)
    s = jnp.where(rows >= cols, s, -jnp.inf)
    p = jnp.exp(s - jnp.max(s, axis=-1, keepdims=True))
    return p / jnp.sum(p, axis=-1, keepdims=True)


def forward_kernel(qkv, copies, ctx, sems):
    blocks = qkv.shape[0] // QB
    out = []
    for i in range(blocks):
        rows, seen = pl.ds(i * QB, QB), pl.ds(0, (i + 1) * QB)
        low = attend_block(qkv[rows, :DH], qkv[seen, DH : 2 * DH], i * QB).astype(BF16)
        ctx[rows, :] = jnp.dot(low, qkv[seen, 2 * DH :], preferred_element_type=F32).astype(BF16)
        for c in range(copies.shape[0]):
            out.append(
                pltpu.make_async_copy(ctx.at[rows, :], copies.at[c, rows, :], sems.at[i, c])
            )
            out[-1].start()
    for copy in out:
        copy.wait()


def backward_kernel(qkv, parts, out, dk, dv):
    blocks = qkv.shape[0] // QB
    step = pl.program_id(0)

    for i in reversed(range(blocks)):

        @pl.when(step == blocks - 1 - i)
        def _(i=i):
            rows, seen = pl.ds(i * QB, QB), pl.ds(0, (i + 1) * QB)
            q, k, v = qkv[rows, :DH], qkv[seen, DH : 2 * DH], qkv[seen, 2 * DH :]
            g = parts[0].astype(F32)
            for c in range(1, parts.shape[0]):
                g = g + parts[c].astype(F32)
            g = g.astype(BF16)
            attend = attend_block(q, k, i * QB)
            dp = lax.dot_general(g, v, NT, preferred_element_type=F32)
            dot = jnp.sum(attend * dp, axis=-1, keepdims=True)
            ds = (attend * (dp - dot) * SCALE).astype(BF16)
            out[:, :DH] = jnp.dot(ds, k, preferred_element_type=F32).astype(BF16)
            dk_part = lax.dot_general(ds, q, TN, preferred_element_type=F32)
            dv_part = lax.dot_general(attend.astype(BF16), g, TN, preferred_element_type=F32)
            if i == blocks - 1:
                dk[...] = dk_part
                dv[...] = dv_part
            else:
                dk[seen, :] += dk_part
                dv[seen, :] += dv_part
            out[:, DH : 2 * DH] = dk[rows, :].astype(BF16)
            out[:, 2 * DH :] = dv[rows, :].astype(BF16)


def context_grad_kernel(grad_all, w, slots, token, part, sems):
    token[...] = jnp.zeros(token.shape, token.dtype)
    leave = []
    for j in range(0, 6, 2):
        both = lax.dot_general(
            grad_all[...], w[j * DH : (j + 2) * DH, :], NT, preferred_element_type=F32
        ).astype(BF16)
        for k in range(2):
            part[j + k] = both[:, k * DH : (k + 1) * DH]
            leave.append(
                pltpu.make_async_copy(part.at[j + k], slots.at[OWNERS[j + k]], sems.at[j + k])
            )
            leave[-1].start()
    for copy in leave:
        copy.wait()


def rows_for(ctx, h, core):
    first = [pl.multiple_of((2 * lax.rem(h + s, 4) + core) * POS, POS) for s in (2, 1, 3, 0)]
    return jnp.concatenate([ctx[pl.ds(f, POS), :] for f in first], axis=0)


def theirs_kernel(place, near, other, weight, ctx, left, right, w, sems_in, sems_w):
    h, core, z = place[0], place[1], place[2]
    wide = left.shape[1]
    lanes = [pl.ds(i * wide, wide) for i in range(2)]
    arrive = []
    for i, (blocks, zz) in enumerate(((near, z), (other, 1 - z))):
        for y in range(3):
            first = pl.multiple_of((3 * zz + y) * DH, DH)
            arrive.append(
                pltpu.make_async_copy(blocks.at[y], ctx.at[:, pl.ds(first, DH)], sems_in.at[i, y])
            )
    weights = [
        pltpu.make_async_copy(weight.at[:, lane], w.at[:, lane], sems_w.at[i])
        for i, lane in enumerate(lanes)
    ]
    for copy in arrive + weights:
        copy.start()
    for copy in arrive:
        copy.wait()
    rows = rows_for(ctx, h, 1 - core)
    for i, out in enumerate((left, right)):
        weights[i].wait()
        out[...] = jnp.dot(rows, w[:, lanes[i]], preferred_element_type=F32).astype(BF16)


def mine_kernel(place, ctx, w, left, right, far, now, later, own, token):
    token[...] = jnp.zeros(token.shape, token.dtype)
    h, core = place[0], place[1]
    rows = rows_for(ctx, h, core)
    wide = left.shape[1]
    for i, theirs in enumerate((left, right)):
        lane = pl.ds(i * wide, wide)
        part = jnp.dot(rows, w[:, lane], preferred_element_type=F32)
        part = part + theirs[...].astype(F32)
        far[:, lane] = part[:POS].astype(BF16)
        up, down = part[POS : 2 * POS], part[2 * POS : 3 * POS]
        now[:, lane] = jnp.where(core == 0, down, up).astype(BF16)
        later[:, lane] = jnp.where(core == 0, up, down)
        own[:, lane] = part[3 * POS :]


def add_kernel(a, *parts):
    total = a[...]
    for part in parts[:-1]:
        total = total + part[...].astype(F32)
    parts[-1][...] = total.astype(BF16)


def weight_kernel(ctx, grad_all, out, token):
    token[...] = jnp.zeros(token.shape, token.dtype)
    out[...] = lax.dot_general(
        ctx[...], grad_all[...], TN, preferred_element_type=F32
    ).astype(out.dtype)


def shards(queries, keys, values, weight, out_grad):
    feats = weight.shape[1]
    seq = 8 * POS
    width = 6 * DH
    steps = seq // QB
    row, col = lax.axis_index("row"), lax.axis_index("col")
    place = jnp.stack([row // 2, row % 2, col // 4]).astype(jnp.int32)
    on_row = lambda a, perm: lax.ppermute(a, "row", perm)
    scalars = pl.BlockSpec(memory_space=pltpu.SMEM)
    trade = lambda a: lax.all_to_all(a, "col", 0, 0, tiled=True)
    whole = lambda shape: pl.BlockSpec(shape, lambda i: (0,) * len(shape))
    lanes_of = lambda rows: pl.BlockSpec((rows, 512), lambda i: (0, i))

    grad_all = lax.all_gather(out_grad, "row", axis=0, tiled=True)

    (slots,) = local(
        pack_kernel, "pack_heads", [((8, POS, 3 * DH), BF16, IN_HBM)], (queries, keys, values)
    )
    qkv = trade(slots).reshape(seq, 3 * DH)

    (copies,) = local(
        forward_kernel,
        "attend_forward",
        [((4, seq, DH), BF16, IN_HBM)],
        (qkv,),
        out_specs=[HBM],
        scratch=[pltpu.VMEM((seq, DH), BF16), pltpu.SemaphoreType.DMA((steps, 4))],
    )
    near = lax.all_to_all(copies, "col", 0, 0, tiled=True, axis_index_groups=SAME_Z)
    other = lax.ppermute(near[:3], "col", ACROSS_Z)

    parts, token = local(
        context_grad_kernel,
        "context_grad",
        [((8, seq, DH), BF16, IN_HBM), ((8, DH), F32, ARRAY)],
        (grad_all, weight),
        out_specs=[HBM, WHOLE],
        scratch=[pltpu.VMEM((6, seq, DH), BF16), pltpu.SemaphoreType.DMA((6,))],
        vmem=24,
    )
    parts = trade(parts)

    ctx, *theirs = local(
        theirs_kernel,
        "project_theirs",
        [((seq, width), BF16, ARRAY)] + [((seq // 2, feats // 2), BF16, ARRAY)] * 2,
        (place, near, other, weight),
        in_specs=[scalars, HBM, HBM, HBM],
        scratch=[
            pltpu.VMEM((width, feats), BF16),
            pltpu.SemaphoreType.DMA((2, 3)),
            pltpu.SemaphoreType.DMA((2,)),
        ],
        after=[token],
        flops=60_000_000_000,
        vmem=24,
    )
    block = (POS, feats)
    far, now, later, own, token = local(
        mine_kernel,
        "project_mine",
        [(block, BF16, ARRAY)] * 2
        + [(block, F32, IN_HBM)] * 2
        + [((8, DH), F32, ARRAY)],
        (place, ctx, weight, *[on_row(a, ACROSS_CORE) for a in theirs]),
        in_specs=[scalars] + [WHOLE] * 4,
        vmem=24,
    )
    far = on_row(far, by_core(1))
    now = on_row(now, by_core(-1))
    (later,) = local(add_kernel, "add_output", [(block, BF16, ARRAY)], (later, far), flops=60_000_000_000, vmem=24)
    later = on_row(later, by_core(1))
    (output,) = local(
        add_kernel,
        "sum_output",
        [(block, BF16, ARRAY)],
        (own, now, later),
        vmem=24,
    )

    w_part, token = local(
        weight_kernel,
        "weight_grad",
        [((width, feats), BF16, IN_HBM), ((8, DH), F32, ARRAY)],
        (ctx, grad_all),
        after=[token],
        vmem=24,
        grid=(feats // 512,),
        in_specs=[whole((seq, width)), lanes_of(seq)],
        out_specs=[lanes_of(width), whole((8, DH))],
    )
    weight_grad = lax.psum_scatter(w_part, "depth", scatter_dimension=0, tiled=True)

    (back,) = local(
        backward_kernel,
        "attend_backward",
        [((seq, 3 * DH), BF16, IN_HBM)],
        (qkv, parts),
        after=[token],
        vmem=24,
        grid=(steps,),
        in_specs=[
            whole((seq, 3 * DH)),
            pl.BlockSpec((8, QB, DH), lambda i: (0, steps - 1 - i, 0)),
        ],
        out_specs=[pl.BlockSpec((QB, 3 * DH), lambda i: (steps - 1 - i, 0))],
        scratch=[pltpu.VMEM((seq, DH), F32), pltpu.VMEM((seq, DH), F32)],
    )
    back = trade(back.reshape(8, POS, 3 * DH))
    grads = local(unpack_kernel, "unpack_heads", [((POS, width), BF16, ARRAY)] * 3, (back,), vmem=24)

    return output, grads[0], grads[1], grads[2], weight_grad


def solution(mesh):
    in_specs = (
        P(("depth", "col"), "row"),
        P(("depth", "col"), "row"),
        P(("depth", "col"), "row"),
        P("row", "col"),
        P(("depth", "row"), "col"),
    )
    out_specs = (
        P(("depth", "row"), "col"),
        P(("depth", "col"), "row"),
        P(("depth", "col"), "row"),
        P(("depth", "col"), "row"),
        P(("row", "depth"), "col"),
    )
    return jax.shard_map(shards, mesh=mesh, in_specs=in_specs, out_specs=out_specs, check_vma=False)
```

```python
import math

import jax
import jax.numpy as jnp
from jax import lax
from jax.experimental import pallas as pl
from jax.experimental.pallas import tpu as pltpu
from jax.sharding import PartitionSpec as P

DH = 128
POS = 128
QB = 256
SCALE = 1.0 / math.sqrt(DH)
F32 = jnp.float32
BF16 = jnp.bfloat16
NT = (((1,), (1,)), ((), ()))
TN = (((0,), (0,)), ((), ()))

OWNERS = (0, 1, 2, 4, 5, 6)

SAME_Z = [[0, 1, 2, 3], [4, 5, 6, 7]]
ACROSS_Z = [(c, (c + 4) % 8) for c in range(8)]
ACROSS_CORE = [(r, r ^ 1) for r in range(8)]


def by_core(step):
    return [(2 * h + k, 2 * ((h + step * (1 - 2 * k)) % 4) + k) for h in range(4) for k in range(2)]


ARRAY = jax.ShapeDtypeStruct
IN_HBM = pltpu.HBM
HBM = pl.BlockSpec(memory_space=pltpu.HBM)
WHOLE = pl.BlockSpec(memory_space=pltpu.VMEM)


def local(kernel, name, outs, args, out_specs=None, in_specs=None, grid=(), scratch=(), after=(), flops=1024, vmem=56):
    count = len(args)

    def body(*refs):
        kernel(*refs[:count], *refs[count + len(after) :])

    return pl.pallas_call(
        body,
        out_shape=[kind(shape, dtype) for shape, dtype, kind in outs],
        grid=grid,
        in_specs=list(in_specs or [WHOLE] * count)
        + [pl.BlockSpec(memory_space=pl.ANY)] * len(after),
        out_specs=list(out_specs or [WHOLE] * len(outs)),
        scratch_shapes=list(scratch),
        compiler_params=pltpu.CompilerParams(vmem_limit_bytes=vmem * 1024 * 1024),
        cost_estimate=pl.CostEstimate(flops=flops, bytes_accessed=1024, transcendentals=0),
        name=name,
    )(*args, *after)


def pack_kernel(q, k, v, slots, sems):
    copies = [
        pltpu.make_async_copy(
            a.at[:, j * DH : (j + 1) * DH],
            slots.at[slot, :, i * DH : (i + 1) * DH],
            sems.at[i, j],
        )
        for i, a in enumerate((q, k, v))
        for j, slot in enumerate(OWNERS)
    ]
    for copy in copies:
        copy.start()
    for copy in copies:
        copy.wait()


def unpack_kernel(slots, q, k, v):
    for j, slot in enumerate(OWNERS):
        for i, a in enumerate((q, k, v)):
            a[:, j * DH : (j + 1) * DH] = slots[slot, :, i * DH : (i + 1) * DH]


def attend_block(q, k, first):
    keys = k.shape[0]
    s = lax.dot_general(q, k, NT, preferred_element_type=F32) * SCALE
    rows = first + lax.broadcasted_iota(jnp.int32, (QB, keys), 0)
    cols = lax.broadcasted_iota(jnp.int32, (QB, keys), 1)
    s = jnp.where(rows >= cols, s, -jnp.inf)
    p = jnp.exp(s - jnp.max(s, axis=-1, keepdims=True))
    return p / jnp.sum(p, axis=-1, keepdims=True)


def forward_kernel(qkv, copies, ctx, sems):
    blocks = qkv.shape[0] // QB
    out = []
    for i in range(blocks):
        rows, seen = pl.ds(i * QB, QB), pl.ds(0, (i + 1) * QB)
        low = attend_block(qkv[rows, :DH], qkv[seen, DH : 2 * DH], i * QB).astype(BF16)
        ctx[rows, :] = jnp.dot(low, qkv[seen, 2 * DH :], preferred_element_type=F32).astype(BF16)
        for c in range(copies.shape[0]):
            out.append(
                pltpu.make_async_copy(ctx.at[rows, :], copies.at[c, rows, :], sems.at[i, c])
            )
            out[-1].start()
    for copy in out:
        copy.wait()


def backward_kernel(qkv, parts, out, dk, dv):
    blocks = qkv.shape[0] // QB
    step = pl.program_id(0)

    for i in reversed(range(blocks)):

        @pl.when(step == blocks - 1 - i)
        def _(i=i):
            rows, seen = pl.ds(i * QB, QB), pl.ds(0, (i + 1) * QB)
            q, k, v = qkv[rows, :DH], qkv[seen, DH : 2 * DH], qkv[seen, 2 * DH :]
            g = parts[0].astype(F32)
            for c in range(1, parts.shape[0]):
                g = g + parts[c].astype(F32)
            g = g.astype(BF16)
            attend = attend_block(q, k, i * QB)
            dp = lax.dot_general(g, v, NT, preferred_element_type=F32)
            dot = jnp.sum(attend * dp, axis=-1, keepdims=True)
            ds = (attend * (dp - dot) * SCALE).astype(BF16)
            out[:, :DH] = jnp.dot(ds, k, preferred_element_type=F32).astype(BF16)
            dk_part = lax.dot_general(ds, q, TN, preferred_element_type=F32)
            dv_part = lax.dot_general(attend.astype(BF16), g, TN, preferred_element_type=F32)
            if i == blocks - 1:
                dk[...] = dk_part
                dv[...] = dv_part
            else:
                dk[seen, :] += dk_part
                dv[seen, :] += dv_part
            out[:, DH : 2 * DH] = dk[rows, :].astype(BF16)
            out[:, 2 * DH :] = dv[rows, :].astype(BF16)


def context_grad_kernel(grad_all, w, slots, token, part, sems):
    token[...] = jnp.zeros(token.shape, token.dtype)
    leave = []
    for j in range(0, 6, 2):
        both = lax.dot_general(
            grad_all[...], w[j * DH : (j + 2) * DH, :], NT, preferred_element_type=F32
        ).astype(BF16)
        for k in range(2):
            part[j + k] = both[:, k * DH : (k + 1) * DH]
            leave.append(
                pltpu.make_async_copy(part.at[j + k], slots.at[OWNERS[j + k]], sems.at[j + k])
            )
            leave[-1].start()
    for copy in leave:
        copy.wait()


def rows_for(ctx, h, core):
    first = [pl.multiple_of((2 * lax.rem(h + s, 4) + core) * POS, POS) for s in (2, 1, 3, 0)]
    return jnp.concatenate([ctx[pl.ds(f, POS), :] for f in first], axis=0)


def theirs_kernel(place, near, other, weight, ctx, left, right, w, sems_in, sems_w):
    h, core, z = place[0], place[1], place[2]
    wide = left.shape[1]
    lanes = [pl.ds(i * wide, wide) for i in range(2)]
    arrive = []
    for i, (blocks, zz) in enumerate(((near, z), (other, 1 - z))):
        for y in range(3):
            first = pl.multiple_of((3 * zz + y) * DH, DH)
            arrive.append(
                pltpu.make_async_copy(blocks.at[y], ctx.at[:, pl.ds(first, DH)], sems_in.at[i, y])
            )
    weights = [
        pltpu.make_async_copy(weight.at[:, lane], w.at[:, lane], sems_w.at[i])
        for i, lane in enumerate(lanes)
    ]
    for copy in arrive + weights:
        copy.start()
    for copy in arrive:
        copy.wait()
    rows = rows_for(ctx, h, 1 - core)
    for i, out in enumerate((left, right)):
        weights[i].wait()
        out[...] = jnp.dot(rows, w[:, lanes[i]], preferred_element_type=F32).astype(BF16)


def mine_kernel(place, ctx, w, left, right, far, now, later, own, token):
    token[...] = jnp.zeros(token.shape, token.dtype)
    h, core = place[0], place[1]
    rows = rows_for(ctx, h, core)
    wide = left.shape[1]
    for i, theirs in enumerate((left, right)):
        lane = pl.ds(i * wide, wide)
        part = jnp.dot(rows, w[:, lane], preferred_element_type=F32)
        part = part + theirs[...].astype(F32)
        far[:, lane] = part[:POS].astype(BF16)
        up, down = part[POS : 2 * POS], part[2 * POS : 3 * POS]
        now[:, lane] = jnp.where(core == 0, down, up).astype(BF16)
        later[:, lane] = jnp.where(core == 0, up, down)
        own[:, lane] = part[3 * POS :]


def add_kernel(a, *parts):
    total = a[...]
    for part in parts[:-1]:
        total = total + part[...].astype(F32)
    parts[-1][...] = total.astype(BF16)


def weight_kernel(ctx, grad_all, out, token):
    token[...] = jnp.zeros(token.shape, token.dtype)
    out[...] = lax.dot_general(
        ctx[...], grad_all[...], TN, preferred_element_type=F32
    ).astype(out.dtype)


def shards(queries, keys, values, weight, out_grad):
    feats = weight.shape[1]
    seq = 8 * POS
    width = 6 * DH
    steps = seq // QB
    row, col = lax.axis_index("row"), lax.axis_index("col")
    place = jnp.stack([row // 2, row % 2, col // 4]).astype(jnp.int32)
    on_row = lambda a, perm: lax.ppermute(a, "row", perm)
    scalars = pl.BlockSpec(memory_space=pltpu.SMEM)
    trade = lambda a: lax.all_to_all(a, "col", 0, 0, tiled=True)
    whole = lambda shape: pl.BlockSpec(shape, lambda i: (0,) * len(shape))
    lanes_of = lambda rows: pl.BlockSpec((rows, 512), lambda i: (0, i))

    grad_all = lax.all_gather(out_grad, "row", axis=0, tiled=True)

    (slots,) = local(
        pack_kernel,
        "pack_heads",
        [((8, POS, 3 * DH), BF16, IN_HBM)],
        (queries, keys, values),
        in_specs=[HBM] * 3,
        out_specs=[HBM],
        scratch=[pltpu.SemaphoreType.DMA((3, 6))],
    )
    qkv = trade(slots).reshape(seq, 3 * DH)

    (copies,) = local(
        forward_kernel,
        "attend_forward",
        [((4, seq, DH), BF16, IN_HBM)],
        (qkv,),
        out_specs=[HBM],
        scratch=[pltpu.VMEM((seq, DH), BF16), pltpu.SemaphoreType.DMA((steps, 4))],
    )
    near = lax.all_to_all(copies, "col", 0, 0, tiled=True, axis_index_groups=SAME_Z)
    other = lax.ppermute(near[:3], "col", ACROSS_Z)

    parts, token = local(
        context_grad_kernel,
        "context_grad",
        [((8, seq, DH), BF16, IN_HBM), ((8, DH), F32, ARRAY)],
        (grad_all, weight),
        out_specs=[HBM, WHOLE],
        scratch=[pltpu.VMEM((6, seq, DH), BF16), pltpu.SemaphoreType.DMA((6,))],
        vmem=24,
    )
    parts = trade(parts)

    ctx, *theirs = local(
        theirs_kernel,
        "project_theirs",
        [((seq, width), BF16, ARRAY)] + [((seq // 2, feats // 2), BF16, ARRAY)] * 2,
        (place, near, other, weight),
        in_specs=[scalars, HBM, HBM, HBM],
        scratch=[
            pltpu.VMEM((width, feats), BF16),
            pltpu.SemaphoreType.DMA((2, 3)),
            pltpu.SemaphoreType.DMA((2,)),
        ],
        after=[token],
        flops=60_000_000_000,
        vmem=24,
    )
    w_part, token = local(
        weight_kernel,
        "weight_grad",
        [((width, feats), BF16, ARRAY), ((8, DH), F32, ARRAY)],
        (ctx, grad_all),
        vmem=24,
        grid=(feats // 512,),
        in_specs=[whole((seq, width)), lanes_of(seq)],
        out_specs=[lanes_of(width), whole((8, DH))],
    )
    weight_grad = lax.psum_scatter(w_part, "depth", scatter_dimension=0, tiled=True)

    block = (POS, feats)
    far, now, later, own, token = local(
        mine_kernel,
        "project_mine",
        [(block, dtype, ARRAY) for dtype in (BF16, BF16, F32, F32)] + [((8, DH), F32, ARRAY)],
        (place, ctx, weight, *[on_row(a, ACROSS_CORE) for a in theirs]),
        in_specs=[scalars] + [WHOLE] * 4,
        after=[token],
        vmem=24,
    )
    far = on_row(far, by_core(1))
    now = on_row(now, by_core(-1))
    (later,) = local(add_kernel, "add_output", [(block, BF16, ARRAY)], (later, far), flops=60_000_000_000, vmem=24)
    later = on_row(later, by_core(1))
    (output,) = local(
        add_kernel,
        "sum_output",
        [(block, BF16, ARRAY)],
        (own, now, later),
        vmem=24,
    )

    (back,) = local(
        backward_kernel,
        "attend_backward",
        [((seq, 3 * DH), BF16, IN_HBM)],
        (qkv, parts),
        after=[token],
        vmem=24,
        grid=(steps,),
        in_specs=[
            whole((seq, 3 * DH)),
            pl.BlockSpec((8, QB, DH), lambda i: (0, steps - 1 - i, 0)),
        ],
        out_specs=[pl.BlockSpec((QB, 3 * DH), lambda i: (steps - 1 - i, 0))],
        scratch=[pltpu.VMEM((seq, DH), F32), pltpu.VMEM((seq, DH), F32)],
    )
    back = trade(back.reshape(8, POS, 3 * DH))
    grads = local(unpack_kernel, "unpack_heads", [((POS, width), BF16, ARRAY)] * 3, (back,), vmem=24)

    return output, grads[0], grads[1], grads[2], weight_grad


def solution(mesh):
    in_specs = (
        P(("depth", "col"), "row"),
        P(("depth", "col"), "row"),
        P(("depth", "col"), "row"),
        P("row", "col"),
        P(("depth", "row"), "col"),
    )
    out_specs = (
        P(("depth", "row"), "col"),
        P(("depth", "col"), "row"),
        P(("depth", "col"), "row"),
        P(("depth", "col"), "row"),
        P(("row", "depth"), "col"),
    )
    return jax.shard_map(shards, mesh=mesh, in_specs=in_specs, out_specs=out_specs, check_vma=False)
```

```python
import math

import jax
import jax.numpy as jnp
from jax import lax
from jax.experimental import pallas as pl
from jax.experimental.pallas import tpu as pltpu
from jax.sharding import PartitionSpec as P

DH = 128
POS = 128
QB = 256
SCALE = 1.0 / math.sqrt(DH)
F32 = jnp.float32
BF16 = jnp.bfloat16
NT = (((1,), (1,)), ((), ()))
TN = (((0,), (0,)), ((), ()))

OWNERS = (0, 1, 2, 4, 5, 6)

SAME_Z = [[0, 1, 2, 3], [4, 5, 6, 7]]
ACROSS_Z = [(c, (c + 4) % 8) for c in range(8)]
ACROSS_CORE = [(r, r ^ 1) for r in range(8)]


def by_core(step):
    return [(2 * h + k, 2 * ((h + step * (1 - 2 * k)) % 4) + k) for h in range(4) for k in range(2)]


ARRAY = jax.ShapeDtypeStruct
IN_HBM = pltpu.HBM
HBM = pl.BlockSpec(memory_space=pltpu.HBM)
WHOLE = pl.BlockSpec(memory_space=pltpu.VMEM)


def local(kernel, name, outs, args, out_specs=None, in_specs=None, grid=(), scratch=(), after=(), flops=1024, vmem=56):
    count = len(args)

    def body(*refs):
        kernel(*refs[:count], *refs[count + len(after) :])

    return pl.pallas_call(
        body,
        out_shape=[kind(shape, dtype) for shape, dtype, kind in outs],
        grid=grid,
        in_specs=list(in_specs or [WHOLE] * count)
        + [pl.BlockSpec(memory_space=pl.ANY)] * len(after),
        out_specs=list(out_specs or [WHOLE] * len(outs)),
        scratch_shapes=list(scratch),
        compiler_params=pltpu.CompilerParams(vmem_limit_bytes=vmem * 1024 * 1024),
        cost_estimate=pl.CostEstimate(flops=flops, bytes_accessed=1024, transcendentals=0),
        name=name,
    )(*args, *after)


def pack_kernel(q, k, v, slots, rows, packed, sems_in, sems_out):
    arrive = [
        pltpu.make_async_copy(a, rows.at[i], sems_in.at[i]) for i, a in enumerate((q, k, v))
    ]
    for copy in arrive:
        copy.start()
    for copy in arrive:
        copy.wait()
    leave = []
    for j, slot in enumerate(OWNERS):
        for i in range(3):
            packed[j, :, i * DH : (i + 1) * DH] = rows[i, :, j * DH : (j + 1) * DH]
        leave.append(pltpu.make_async_copy(packed.at[j], slots.at[slot], sems_out.at[j]))
        leave[-1].start()
    for copy in leave:
        copy.wait()


def unpack_kernel(slots, q, k, v):
    for j, slot in enumerate(OWNERS):
        for i, a in enumerate((q, k, v)):
            a[:, j * DH : (j + 1) * DH] = slots[slot, :, i * DH : (i + 1) * DH]


def attend_block(q, k, first):
    keys = k.shape[0]
    s = lax.dot_general(q, k, NT, preferred_element_type=F32) * SCALE
    rows = first + lax.broadcasted_iota(jnp.int32, (QB, keys), 0)
    cols = lax.broadcasted_iota(jnp.int32, (QB, keys), 1)
    s = jnp.where(rows >= cols, s, -jnp.inf)
    p = jnp.exp(s - jnp.max(s, axis=-1, keepdims=True))
    return p / jnp.sum(p, axis=-1, keepdims=True)


def forward_kernel(qkv, copies, ctx, sems):
    blocks = qkv.shape[0] // QB
    out = []
    for i in range(blocks):
        rows, seen = pl.ds(i * QB, QB), pl.ds(0, (i + 1) * QB)
        low = attend_block(qkv[rows, :DH], qkv[seen, DH : 2 * DH], i * QB).astype(BF16)
        ctx[rows, :] = jnp.dot(low, qkv[seen, 2 * DH :], preferred_element_type=F32).astype(BF16)
        for c in range(copies.shape[0]):
            out.append(
                pltpu.make_async_copy(ctx.at[rows, :], copies.at[c, rows, :], sems.at[i, c])
            )
            out[-1].start()
    for copy in out:
        copy.wait()


def backward_kernel(qkv, parts, out, dk, dv):
    blocks = qkv.shape[0] // QB
    step = pl.program_id(0)

    for i in reversed(range(blocks)):

        @pl.when(step == blocks - 1 - i)
        def _(i=i):
            rows, seen = pl.ds(i * QB, QB), pl.ds(0, (i + 1) * QB)
            q, k, v = qkv[rows, :DH], qkv[seen, DH : 2 * DH], qkv[seen, 2 * DH :]
            g = parts[0].astype(F32)
            for c in range(1, parts.shape[0]):
                g = g + parts[c].astype(F32)
            g = g.astype(BF16)
            attend = attend_block(q, k, i * QB)
            dp = lax.dot_general(g, v, NT, preferred_element_type=F32)
            dot = jnp.sum(attend * dp, axis=-1, keepdims=True)
            ds = (attend * (dp - dot) * SCALE).astype(BF16)
            out[:, :DH] = jnp.dot(ds, k, preferred_element_type=F32).astype(BF16)
            dk_part = lax.dot_general(ds, q, TN, preferred_element_type=F32)
            dv_part = lax.dot_general(attend.astype(BF16), g, TN, preferred_element_type=F32)
            if i == blocks - 1:
                dk[...] = dk_part
                dv[...] = dv_part
            else:
                dk[seen, :] += dk_part
                dv[seen, :] += dv_part
            out[:, DH : 2 * DH] = dk[rows, :].astype(BF16)
            out[:, 2 * DH :] = dv[rows, :].astype(BF16)


def context_grad_kernel(grad_all, w, slots, token, part, sems):
    token[...] = jnp.zeros(token.shape, token.dtype)
    leave = []
    for j in range(0, 6, 2):
        both = lax.dot_general(
            grad_all[...], w[j * DH : (j + 2) * DH, :], NT, preferred_element_type=F32
        ).astype(BF16)
        for k in range(2):
            part[j + k] = both[:, k * DH : (k + 1) * DH]
            leave.append(
                pltpu.make_async_copy(part.at[j + k], slots.at[OWNERS[j + k]], sems.at[j + k])
            )
            leave[-1].start()
    for copy in leave:
        copy.wait()


def rows_for(ctx, h, core):
    first = [pl.multiple_of((2 * lax.rem(h + s, 4) + core) * POS, POS) for s in (2, 1, 3, 0)]
    return jnp.concatenate([ctx[pl.ds(f, POS), :] for f in first], axis=0)


def theirs_kernel(place, near, other, weight, ctx, left, right, w, sems_in, sems_w):
    h, core, z = place[0], place[1], place[2]
    wide = left.shape[1]
    lanes = [pl.ds(i * wide, wide) for i in range(2)]
    arrive = []
    for i, (blocks, zz) in enumerate(((near, z), (other, 1 - z))):
        for y in range(3):
            first = pl.multiple_of((3 * zz + y) * DH, DH)
            arrive.append(
                pltpu.make_async_copy(blocks.at[y], ctx.at[:, pl.ds(first, DH)], sems_in.at[i, y])
            )
    weights = [
        pltpu.make_async_copy(weight.at[:, lane], w.at[:, lane], sems_w.at[i])
        for i, lane in enumerate(lanes)
    ]
    for copy in arrive + weights:
        copy.start()
    for copy in arrive:
        copy.wait()
    rows = rows_for(ctx, h, 1 - core)
    for i, out in enumerate((left, right)):
        weights[i].wait()
        out[...] = jnp.dot(rows, w[:, lanes[i]], preferred_element_type=F32).astype(BF16)


def mine_kernel(place, ctx, w, left, right, far, now, later, own, token):
    token[...] = jnp.zeros(token.shape, token.dtype)
    h, core = place[0], place[1]
    rows = rows_for(ctx, h, core)
    wide = left.shape[1]
    for i, theirs in enumerate((left, right)):
        lane = pl.ds(i * wide, wide)
        part = jnp.dot(rows, w[:, lane], preferred_element_type=F32)
        part = part + theirs[...].astype(F32)
        far[:, lane] = part[:POS].astype(BF16)
        up, down = part[POS : 2 * POS], part[2 * POS : 3 * POS]
        now[:, lane] = jnp.where(core == 0, down, up).astype(BF16)
        later[:, lane] = jnp.where(core == 0, up, down)
        own[:, lane] = part[3 * POS :]


def add_kernel(a, *parts):
    total = a[...]
    for part in parts[:-1]:
        total = total + part[...].astype(F32)
    parts[-1][...] = total.astype(BF16)


def weight_kernel(ctx, grad_all, out, token):
    token[...] = jnp.zeros(token.shape, token.dtype)
    out[...] = lax.dot_general(
        ctx[...], grad_all[...], TN, preferred_element_type=F32
    ).astype(out.dtype)


def shards(queries, keys, values, weight, out_grad):
    feats = weight.shape[1]
    seq = 8 * POS
    width = 6 * DH
    steps = seq // QB
    row, col = lax.axis_index("row"), lax.axis_index("col")
    place = jnp.stack([row // 2, row % 2, col // 4]).astype(jnp.int32)
    on_row = lambda a, perm: lax.ppermute(a, "row", perm)
    scalars = pl.BlockSpec(memory_space=pltpu.SMEM)
    trade = lambda a: lax.all_to_all(a, "col", 0, 0, tiled=True)
    whole = lambda shape: pl.BlockSpec(shape, lambda i: (0,) * len(shape))
    lanes_of = lambda rows: pl.BlockSpec((rows, 512), lambda i: (0, i))

    grad_all = lax.all_gather(out_grad, "row", axis=0, tiled=True)

    (slots,) = local(
        pack_kernel,
        "pack_heads",
        [((8, POS, 3 * DH), BF16, IN_HBM)],
        (queries, keys, values),
        in_specs=[HBM] * 3,
        out_specs=[HBM],
        scratch=[
            pltpu.VMEM((3, POS, width), BF16),
            pltpu.VMEM((6, POS, 3 * DH), BF16),
            pltpu.SemaphoreType.DMA((3,)),
            pltpu.SemaphoreType.DMA((6,)),
        ],
    )
    qkv = trade(slots).reshape(seq, 3 * DH)

    (copies,) = local(
        forward_kernel,
        "attend_forward",
        [((4, seq, DH), BF16, IN_HBM)],
        (qkv,),
        out_specs=[HBM],
        scratch=[pltpu.VMEM((seq, DH), BF16), pltpu.SemaphoreType.DMA((steps, 4))],
    )
    near = lax.all_to_all(copies, "col", 0, 0, tiled=True, axis_index_groups=SAME_Z)
    other = lax.ppermute(near[:3], "col", ACROSS_Z)

    parts, token = local(
        context_grad_kernel,
        "context_grad",
        [((8, seq, DH), BF16, IN_HBM), ((8, DH), F32, ARRAY)],
        (grad_all, weight),
        out_specs=[HBM, WHOLE],
        scratch=[pltpu.VMEM((6, seq, DH), BF16), pltpu.SemaphoreType.DMA((6,))],
        vmem=24,
    )
    parts = trade(parts)

    ctx, *theirs = local(
        theirs_kernel,
        "project_theirs",
        [((seq, width), BF16, ARRAY)] + [((seq // 2, feats // 2), BF16, ARRAY)] * 2,
        (place, near, other, weight),
        in_specs=[scalars, HBM, HBM, HBM],
        scratch=[
            pltpu.VMEM((width, feats), BF16),
            pltpu.SemaphoreType.DMA((2, 3)),
            pltpu.SemaphoreType.DMA((2,)),
        ],
        after=[token],
        flops=60_000_000_000,
        vmem=24,
    )
    w_part, token = local(
        weight_kernel,
        "weight_grad",
        [((width, feats), BF16, ARRAY), ((8, DH), F32, ARRAY)],
        (ctx, grad_all),
        vmem=24,
        grid=(feats // 512,),
        in_specs=[whole((seq, width)), lanes_of(seq)],
        out_specs=[lanes_of(width), whole((8, DH))],
    )
    weight_grad = lax.psum_scatter(w_part, "depth", scatter_dimension=0, tiled=True)

    block = (POS, feats)
    far, now, later, own, token = local(
        mine_kernel,
        "project_mine",
        [(block, dtype, ARRAY) for dtype in (BF16, BF16, F32, F32)] + [((8, DH), F32, ARRAY)],
        (place, ctx, weight, *[on_row(a, ACROSS_CORE) for a in theirs]),
        in_specs=[scalars] + [WHOLE] * 4,
        after=[token],
        vmem=24,
    )
    far = on_row(far, by_core(1))
    now = on_row(now, by_core(-1))
    (later,) = local(add_kernel, "add_output", [(block, BF16, ARRAY)], (later, far), flops=60_000_000_000, vmem=24)
    later = on_row(later, by_core(1))
    (output,) = local(
        add_kernel,
        "sum_output",
        [(block, BF16, ARRAY)],
        (own, now, later),
        vmem=24,
    )

    (back,) = local(
        backward_kernel,
        "attend_backward",
        [((seq, 3 * DH), BF16, IN_HBM)],
        (qkv, parts),
        after=[token],
        vmem=24,
        grid=(steps,),
        in_specs=[
            whole((seq, 3 * DH)),
            pl.BlockSpec((8, QB, DH), lambda i: (0, steps - 1 - i, 0)),
        ],
        out_specs=[pl.BlockSpec((QB, 3 * DH), lambda i: (steps - 1 - i, 0))],
        scratch=[pltpu.VMEM((seq, DH), F32), pltpu.VMEM((seq, DH), F32)],
    )
    back = trade(back.reshape(8, POS, 3 * DH))
    grads = local(unpack_kernel, "unpack_heads", [((POS, width), BF16, ARRAY)] * 3, (back,), vmem=24)

    return output, grads[0], grads[1], grads[2], weight_grad


def solution(mesh):
    in_specs = (
        P(("depth", "col"), "row"),
        P(("depth", "col"), "row"),
        P(("depth", "col"), "row"),
        P("row", "col"),
        P(("depth", "row"), "col"),
    )
    out_specs = (
        P(("depth", "row"), "col"),
        P(("depth", "col"), "row"),
        P(("depth", "col"), "row"),
        P(("depth", "col"), "row"),
        P(("row", "depth"), "col"),
    )
    return jax.shard_map(shards, mesh=mesh, in_specs=in_specs, out_specs=out_specs, check_vma=False)
```

```python
import math

import jax
import jax.numpy as jnp
from jax import lax
from jax.experimental import pallas as pl
from jax.experimental.pallas import tpu as pltpu
from jax.sharding import PartitionSpec as P

DH = 128
POS = 128
QB = 256
SCALE = 1.0 / math.sqrt(DH)
F32 = jnp.float32
BF16 = jnp.bfloat16
NT = (((1,), (1,)), ((), ()))
TN = (((0,), (0,)), ((), ()))

OWNERS = (0, 1, 2, 4, 5, 6)

SAME_Z = [[0, 1, 2, 3], [4, 5, 6, 7]]
ACROSS_Z = [(c, (c + 4) % 8) for c in range(8)]
ACROSS_CORE = [(r, r ^ 1) for r in range(8)]


def by_core(step):
    return [(2 * h + k, 2 * ((h + step * (1 - 2 * k)) % 4) + k) for h in range(4) for k in range(2)]


ARRAY = jax.ShapeDtypeStruct
IN_HBM = pltpu.HBM
HBM = pl.BlockSpec(memory_space=pltpu.HBM)
WHOLE = pl.BlockSpec(memory_space=pltpu.VMEM)


def local(kernel, name, outs, args, out_specs=None, in_specs=None, grid=(), scratch=(), after=(), flops=1024, vmem=56):
    count = len(args)

    def body(*refs):
        kernel(*refs[:count], *refs[count + len(after) :])

    return pl.pallas_call(
        body,
        out_shape=[kind(shape, dtype) for shape, dtype, kind in outs],
        grid=grid,
        in_specs=list(in_specs or [WHOLE] * count)
        + [pl.BlockSpec(memory_space=pl.ANY)] * len(after),
        out_specs=list(out_specs or [WHOLE] * len(outs)),
        scratch_shapes=list(scratch),
        compiler_params=pltpu.CompilerParams(vmem_limit_bytes=vmem * 1024 * 1024),
        cost_estimate=pl.CostEstimate(flops=flops, bytes_accessed=1024, transcendentals=0),
        name=name,
    )(*args, *after)


def pack_kernel(q, k, v, slots):
    for j, slot in enumerate(OWNERS):
        for i, a in enumerate((q, k, v)):
            slots[slot, :, i * DH : (i + 1) * DH] = a[:, j * DH : (j + 1) * DH]
    for slot in (3, 7):
        slots[slot] = jnp.zeros(slots.shape[1:], slots.dtype)


def unpack_kernel(slots, q, k, v):
    for j, slot in enumerate(OWNERS):
        for i, a in enumerate((q, k, v)):
            a[:, j * DH : (j + 1) * DH] = slots[slot, :, i * DH : (i + 1) * DH]


def attend_block(q, k, first):
    keys = k.shape[0]
    s = lax.dot_general(q, k, NT, preferred_element_type=F32) * SCALE
    rows = first + lax.broadcasted_iota(jnp.int32, (QB, keys), 0)
    cols = lax.broadcasted_iota(jnp.int32, (QB, keys), 1)
    s = jnp.where(rows >= cols, s, -jnp.inf)
    p = jnp.exp(s - jnp.max(s, axis=-1, keepdims=True))
    return p / jnp.sum(p, axis=-1, keepdims=True)


def forward_kernel(qkv, copies, ctx, sems):
    blocks = qkv.shape[0] // QB
    out = []
    for i in range(blocks):
        rows, seen = pl.ds(i * QB, QB), pl.ds(0, (i + 1) * QB)
        low = attend_block(qkv[rows, :DH], qkv[seen, DH : 2 * DH], i * QB).astype(BF16)
        ctx[rows, :] = jnp.dot(low, qkv[seen, 2 * DH :], preferred_element_type=F32).astype(BF16)
        for c in range(copies.shape[0]):
            out.append(
                pltpu.make_async_copy(ctx.at[rows, :], copies.at[c, rows, :], sems.at[i, c])
            )
            out[-1].start()
    for copy in out:
        copy.wait()


def backward_kernel(qkv, parts, out, dk, dv):
    blocks = qkv.shape[0] // QB
    step = pl.program_id(0)

    for i in reversed(range(blocks)):

        @pl.when(step == blocks - 1 - i)
        def _(i=i):
            rows, seen = pl.ds(i * QB, QB), pl.ds(0, (i + 1) * QB)
            q, k, v = qkv[rows, :DH], qkv[seen, DH : 2 * DH], qkv[seen, 2 * DH :]
            g = parts[0].astype(F32)
            for c in range(1, parts.shape[0]):
                g = g + parts[c].astype(F32)
            g = g.astype(BF16)
            attend = attend_block(q, k, i * QB)
            dp = lax.dot_general(g, v, NT, preferred_element_type=F32)
            dot = jnp.sum(attend * dp, axis=-1, keepdims=True)
            ds = (attend * (dp - dot) * SCALE).astype(BF16)
            out[rows, :DH] = jnp.dot(ds, k, preferred_element_type=F32).astype(BF16)
            dk_part = lax.dot_general(ds, q, TN, preferred_element_type=F32)
            dv_part = lax.dot_general(attend.astype(BF16), g, TN, preferred_element_type=F32)
            if i == blocks - 1:
                dk[...] = dk_part
                dv[...] = dv_part
            else:
                dk[seen, :] += dk_part
                dv[seen, :] += dv_part
            out[rows, DH : 2 * DH] = dk[rows, :].astype(BF16)
            out[rows, 2 * DH :] = dv[rows, :].astype(BF16)


def context_grad_kernel(grad_all, w, slots, token, part, sems):
    token[...] = jnp.zeros(token.shape, token.dtype)
    leave = []
    for j in range(0, 6, 2):
        both = lax.dot_general(
            grad_all[...], w[j * DH : (j + 2) * DH, :], NT, preferred_element_type=F32
        ).astype(BF16)
        for k in range(2):
            part[j + k] = both[:, k * DH : (k + 1) * DH]
            leave.append(
                pltpu.make_async_copy(part.at[j + k], slots.at[OWNERS[j + k]], sems.at[j + k])
            )
            leave[-1].start()
    for copy in leave:
        copy.wait()


def rows_for(ctx, h, core):
    first = [pl.multiple_of((2 * lax.rem(h + s, 4) + core) * POS, POS) for s in (2, 1, 3, 0)]
    return jnp.concatenate([ctx[pl.ds(f, POS), :] for f in first], axis=0)


def theirs_kernel(place, near, other, weight, ctx, left, right, w, sems_in, sems_w):
    h, core, z = place[0], place[1], place[2]
    wide = left.shape[1]
    lanes = [pl.ds(i * wide, wide) for i in range(2)]
    arrive = []
    for i, (blocks, zz) in enumerate(((near, z), (other, 1 - z))):
        for y in range(3):
            first = pl.multiple_of((3 * zz + y) * DH, DH)
            arrive.append(
                pltpu.make_async_copy(blocks.at[y], ctx.at[:, pl.ds(first, DH)], sems_in.at[i, y])
            )
    weights = [
        pltpu.make_async_copy(weight.at[:, lane], w.at[:, lane], sems_w.at[i])
        for i, lane in enumerate(lanes)
    ]
    for copy in arrive + weights:
        copy.start()
    for copy in arrive:
        copy.wait()
    rows = rows_for(ctx, h, 1 - core)
    for i, out in enumerate((left, right)):
        weights[i].wait()
        out[...] = jnp.dot(rows, w[:, lanes[i]], preferred_element_type=F32).astype(BF16)


def mine_kernel(place, ctx, w, left, right, far, now, later, own, token):
    token[...] = jnp.zeros(token.shape, token.dtype)
    h, core = place[0], place[1]
    rows = rows_for(ctx, h, core)
    wide = left.shape[1]
    for i, theirs in enumerate((left, right)):
        lane = pl.ds(i * wide, wide)
        part = jnp.dot(rows, w[:, lane], preferred_element_type=F32)
        part = part + theirs[...].astype(F32)
        far[:, lane] = part[:POS].astype(BF16)
        up, down = part[POS : 2 * POS], part[2 * POS : 3 * POS]
        now[:, lane] = jnp.where(core == 0, down, up).astype(BF16)
        later[:, lane] = jnp.where(core == 0, up, down)
        own[:, lane] = part[3 * POS :]


def add_kernel(a, *parts):
    total = a[...]
    for part in parts[:-1]:
        total = total + part[...].astype(F32)
    parts[-1][...] = total.astype(BF16)


def weight_kernel(ctx, grad_all, out, token):
    token[...] = jnp.zeros(token.shape, token.dtype)
    out[...] = lax.dot_general(
        ctx[...], grad_all[...], TN, preferred_element_type=F32
    ).astype(out.dtype)


def shards(queries, keys, values, weight, out_grad):
    feats = weight.shape[1]
    seq = 8 * POS
    width = 6 * DH
    steps = seq // QB
    row, col = lax.axis_index("row"), lax.axis_index("col")
    place = jnp.stack([row // 2, row % 2, col // 4]).astype(jnp.int32)
    on_row = lambda a, perm: lax.ppermute(a, "row", perm)
    scalars = pl.BlockSpec(memory_space=pltpu.SMEM)
    trade = lambda a: lax.all_to_all(a, "col", 0, 0, tiled=True)
    whole = lambda shape: pl.BlockSpec(shape, lambda i: (0,) * len(shape))
    lanes_of = lambda rows: pl.BlockSpec((rows, 512), lambda i: (0, i))

    grad_all = lax.all_gather(out_grad, "row", axis=0, tiled=True)

    (slots,) = local(
        pack_kernel, "pack_heads", [((8, POS, 3 * DH), BF16, IN_HBM)], (queries, keys, values)
    )
    qkv = trade(slots).reshape(seq, 3 * DH)

    (copies,) = local(
        forward_kernel,
        "attend_forward",
        [((4, seq, DH), BF16, IN_HBM)],
        (qkv,),
        out_specs=[HBM],
        scratch=[pltpu.VMEM((seq, DH), BF16), pltpu.SemaphoreType.DMA((steps, 4))],
        vmem=24,
    )
    near = lax.all_to_all(copies, "col", 0, 0, tiled=True, axis_index_groups=SAME_Z)
    other = lax.ppermute(near[:3], "col", ACROSS_Z)

    parts, token = local(
        context_grad_kernel,
        "context_grad",
        [((8, seq, DH), BF16, IN_HBM), ((8, DH), F32, ARRAY)],
        (grad_all, weight),
        out_specs=[HBM, WHOLE],
        scratch=[pltpu.VMEM((6, seq, DH), BF16), pltpu.SemaphoreType.DMA((6,))],
        vmem=24,
    )
    parts = trade(parts)

    ctx, *theirs = local(
        theirs_kernel,
        "project_theirs",
        [((seq, width), BF16, ARRAY)] + [((seq // 2, feats // 2), BF16, ARRAY)] * 2,
        (place, near, other, weight),
        in_specs=[scalars, HBM, HBM, HBM],
        scratch=[
            pltpu.VMEM((width, feats), BF16),
            pltpu.SemaphoreType.DMA((2, 3)),
            pltpu.SemaphoreType.DMA((2,)),
        ],
        after=[token],
        flops=60_000_000_000,
        vmem=24,
    )
    w_part, token = local(
        weight_kernel,
        "weight_grad",
        [((width, feats), BF16, ARRAY), ((8, DH), F32, ARRAY)],
        (ctx, grad_all),
        vmem=24,
        grid=(feats // 512,),
        in_specs=[whole((seq, width)), lanes_of(seq)],
        out_specs=[lanes_of(width), whole((8, DH))],
    )
    weight_grad = lax.psum_scatter(w_part, "depth", scatter_dimension=0, tiled=True)

    block = (POS, feats)
    far, now, later, own, token = local(
        mine_kernel,
        "project_mine",
        [(block, dtype, ARRAY) for dtype in (BF16, BF16, F32, F32)] + [((8, DH), F32, ARRAY)],
        (place, ctx, weight, *[on_row(a, ACROSS_CORE) for a in theirs]),
        in_specs=[scalars] + [WHOLE] * 4,
        after=[token],
        vmem=24,
    )
    far = on_row(far, by_core(1))
    now = on_row(now, by_core(-1))
    (later,) = local(add_kernel, "add_output", [(block, BF16, ARRAY)], (later, far), flops=60_000_000_000, vmem=24)
    later = on_row(later, by_core(1))
    (output,) = local(
        add_kernel,
        "sum_output",
        [(block, BF16, ARRAY)],
        (own, now, later),
        vmem=24,
    )

    (back,) = local(
        backward_kernel,
        "attend_backward",
        [((seq, 3 * DH), BF16, IN_HBM)],
        (qkv, parts),
        after=[token],
        vmem=24,
        grid=(steps,),
        in_specs=[
            whole((seq, 3 * DH)),
            pl.BlockSpec((8, QB, DH), lambda i: (0, steps - 1 - i, 0)),
        ],
        out_specs=[whole((seq, 3 * DH))],
        scratch=[pltpu.VMEM((seq, DH), F32), pltpu.VMEM((seq, DH), F32)],
    )
    back = trade(back.reshape(8, POS, 3 * DH))
    grads = local(unpack_kernel, "unpack_heads", [((POS, width), BF16, ARRAY)] * 3, (back,), vmem=24)

    return output, grads[0], grads[1], grads[2], weight_grad


def solution(mesh):
    in_specs = (
        P(("depth", "col"), "row"),
        P(("depth", "col"), "row"),
        P(("depth", "col"), "row"),
        P("row", "col"),
        P(("depth", "row"), "col"),
    )
    out_specs = (
        P(("depth", "row"), "col"),
        P(("depth", "col"), "row"),
        P(("depth", "col"), "row"),
        P(("depth", "col"), "row"),
        P(("row", "depth"), "col"),
    )
    return jax.shard_map(shards, mesh=mesh, in_specs=in_specs, out_specs=out_specs, check_vma=False)
```
